32 devices in a mesh: groups: 2 (over y), row: 8 (over z, x), col: 2 (over core).
Axes of the slice: x: 2, y: 2, z: 4, core: 2. Of those that a mesh axis runs over, the one named last changes fastest.
Arguments:
- hidden_states: bfloat16 [32, 6144], P(('groups', 'row'), 'col'), parts along dimension 0, may hold values from -6 to 6
- scale_attn: float32 [6144], P('col'), may hold values from 0.5 to 1.5
- w_qkv: bfloat16 [6144, 18432], P('col', 'row'), may hold values from -0.078125 to 0.078125
- w_out: bfloat16 [6144, 6144], P('col', 'row'), may hold values from -0.078125 to 0.078125
- scale_mlp: float32 [6144], P('col'), may hold values from 0.5 to 1.5
- w_gate: bfloat16 [6144, 24576], P('col', 'row'), may hold values from -0.078125 to 0.078125
- w_up: bfloat16 [6144, 24576], P('col', 'row'), may hold values from -0.078125 to 0.078125
- w_down: bfloat16 [24576, 6144], P('row', 'col'), may hold values from -0.0390625 to 0.0390625
Outputs:
- updated: bfloat16 [32, 6144], P(('groups', 'row'), 'col'), parts along dimension 0
The draws below stay inside these ranges and needn't reach their ends.
There are 2 independent parts, one for each index of `groups`. The reference program is written for one: setup_inputs(seed, part) draws one part's arguments, and reference() takes and returns one part's arrays. A program takes and returns all parts, laid end to end along the dimension named above; an argument that names none is the same for every part. Nothing has to cross between parts.
All inputs are finite; a program needn't handle non-finite values.
Results may differ from the reference program's by a relative error of at most 0.015.
Values may be sent and summed in bfloat16 or wider, within the bound.
No kernel may reach another device: no remote copies, remote signals or barrier semaphores. Data moves between devices by JAX's collectives and lax.ppermute only.
A program may use at most 192 MiB of HBM per device.

```python
import math
import jax
import jax.numpy as jnp
from jax import lax

HEADS = 48
HS = 128
D = 6144
FF = 24576
TOKENS = 16
N_COL = 2


def steps_of(key, dims, split, smallest, high):
    def one(dim, blocks):
        steps = jax.random.uniform(jax.random.fold_in(jax.random.fold_in(key, 6), dim), (blocks,), jnp.float32, smallest / len(split), high / len(split))
        return jnp.repeat(jnp.exp(steps), dims[dim] // blocks).reshape((-1,) + (1,) * (len(dims) - dim - 1))

    factor_of = one(*split[0])
    for cut in split[1:]:
        factor_of = factor_of * one(*cut)
    return factor_of


def scatter_about(own_key, dims, deviation, limit, cuts=(), held_as=jnp.bfloat16):
    values = jax.random.normal(own_key, dims, jnp.float32) * deviation
    if len(cuts) > 0:
        values = steps_of(own_key, dims, cuts, -0.22, 0.18) * values
    return jnp.clip(values, min=-limit, max=limit).astype(held_as)


def setup_inputs(seed: int = 0, part: int = 0) -> dict:
    splits = jax.random.split(jax.random.key(seed), 9)
    part_splits = jax.random.split(jax.random.fold_in(splits[8], part), 9)
    hidden_states = scatter_about(part_splits[0], (TOKENS, D), 1.0, 6.0, ((0, 8), (1, 2)))
    scale_attn = jnp.clip(0.5 + 1.0 * jax.random.uniform(splits[1], (D,), jnp.float32) ** steps_of(splits[1], (D,), ((0, 2),), -0.2, 0.2), 0.5, 1.5)
    w_qkv = scatter_about(splits[2], (D, 3 * D), D ** -0.5, 0.078125, ((0, 2), (1, 8)))
    w_out = scatter_about(splits[3], (D, D), D ** -0.5, 0.078125, ((0, 2), (1, 8)))
    scale_mlp = jnp.clip(0.5 + 1.0 * jax.random.uniform(splits[4], (D,), jnp.float32) ** steps_of(splits[4], (D,), ((0, 2),), -0.2, 0.2), 0.5, 1.5)
    w_gate = scatter_about(splits[5], (D, FF), D ** -0.5, 0.078125, ((0, 2), (1, 8)))
    w_up = scatter_about(splits[6], (D, FF), D ** -0.5, 0.078125, ((0, 2), (1, 8)))
    w_down = scatter_about(splits[7], (FF, D), FF ** -0.5, 0.0390625, ((0, 8), (1, 2)))
    return {"hidden_states": hidden_states, "scale_attn": scale_attn, "w_qkv": w_qkv, "w_out": w_out, "scale_mlp": scale_mlp, "w_gate": w_gate, "w_up": w_up, "w_down": w_down}


EPSILON = 1e-06

def normalize(values, scale):
    mean_sq = lax.optimization_barrier(jnp.mean(values * values, axis=-1, keepdims=True))
    return (values * lax.rsqrt(mean_sq + EPSILON) * scale).astype(jnp.bfloat16)

def attend_head(triple):
    queries, key_rows, value_rows = triple
    scores = jnp.dot(queries, key_rows.T, preferred_element_type=jnp.float32) * (1.0 / math.sqrt(HS))
    peak = lax.optimization_barrier(jnp.max(scores, axis=-1, keepdims=True))
    weights = jnp.exp(scores - peak)
    mass = lax.optimization_barrier(jnp.sum(weights, axis=-1, keepdims=True))
    return jnp.dot(weights.astype(jnp.bfloat16), value_rows, preferred_element_type=jnp.float32) / mass

def reference(hidden_states, scale_attn, w_qkv, w_out, scale_mlp, w_gate, w_up, w_down):
    stream = hidden_states.astype(jnp.float32)
    normed = normalize(stream, scale_attn)
    qkv = jnp.dot(normed, w_qkv, preferred_element_type=jnp.float32).astype(jnp.bfloat16)
    arranged = qkv.reshape(TOKENS, N_COL, 3, HEADS // N_COL, HS)

    def heads_of(which):
        return arranged[:, :, which].reshape(TOKENS, HEADS, HS).transpose(1, 0, 2)
    attended = lax.map(attend_head, (heads_of(0), heads_of(1), heads_of(2)))
    attended = attended.transpose(1, 0, 2).reshape(TOKENS, HEADS * HS).astype(jnp.bfloat16)
    attn_out = jnp.dot(attended, w_out, preferred_element_type=jnp.float32).astype(jnp.bfloat16)
    resid = stream + attn_out.astype(jnp.float32)
    normed2 = normalize(resid, scale_mlp)
    gate = jnp.dot(normed2, w_gate, preferred_element_type=jnp.float32)
    upward = jnp.dot(normed2, w_up, preferred_element_type=jnp.float32)
    hidden = (jax.nn.silu(gate) * upward).astype(jnp.bfloat16)
    lowered = jnp.dot(hidden, w_down, preferred_element_type=jnp.float32)
    return (resid + lowered).astype(jnp.bfloat16)
```

```python
import math

import jax
import jax.numpy as jnp
from jax import lax
from jax.sharding import PartitionSpec as P

HEADS = 48
HS = 128
D = 6144


EPSILON = 1e-06


def project(section, weight):
    return jnp.dot(section, weight, preferred_element_type=jnp.float32)


def to_rows(partial_sum, tok_rows):
    groups = lax.axis_size("col")
    row_count = lax.axis_size("row")
    half_rows = tok_rows // groups
    columns = partial_sum.shape[1]
    ordered = (
        partial_sum.reshape(row_count, groups, half_rows, columns)
        .transpose(1, 0, 2, 3)
        .reshape(-1, columns)
    )
    summed = lax.psum_scatter(ordered.astype(jnp.bfloat16), "col", scatter_dimension=0, tiled=True)
    return lax.all_to_all(
        lax.all_to_all(summed, "row", split_axis=0, concat_axis=1, tiled=True),
        "col",
        split_axis=1,
        concat_axis=0,
        tiled=True,
    )


def per_device(hidden_states, scale_attn, w_qkv, w_out, scale_mlp, w_gate, w_up, w_down):
    tok_rows = hidden_states.shape[0]
    groups = lax.axis_size("col")
    stream = hidden_states.astype(jnp.float32)
    totals = lax.psum(jnp.sum(stream * stream, axis=-1), "col")
    normed = (stream * lax.rsqrt(totals / D + EPSILON)[:, None] * scale_attn).astype(jnp.bfloat16)
    qkv_partial = project(lax.all_gather(normed, "row", axis=0, tiled=True), weight=w_qkv)
    qkv = to_rows(qkv_partial, tok_rows)
    local_heads = HEADS // groups
    head_cols = local_heads * HS
    queries = qkv[:, :head_cols].reshape(tok_rows, local_heads, HS)
    key_rows = qkv[:, head_cols : 2 * head_cols]
    value_rows = qkv[:, 2 * head_cols :]
    factor = 1.0 / math.sqrt(HS)
    running = jnp.full((local_heads, tok_rows), -1e30, jnp.float32)
    key_piece = lax.all_gather(key_rows, "row", axis=0, tiled=True).reshape(-1, local_heads, HS)
    value_piece = lax.all_gather(value_rows, "row", axis=0, tiled=True).reshape(-1, local_heads, HS)
    scores = (
        jnp.einsum("qhd,khd->hqk", queries, key_piece, preferred_element_type=jnp.float32) * factor
    )
    new_max = jnp.maximum(running, jnp.max(scores, axis=-1))
    weights = jnp.exp(scores - new_max[..., None])
    weight_sum = jnp.sum(weights, axis=-1)
    numerator = jnp.einsum(
        "hqk,khd->hqd",
        weights.astype(jnp.bfloat16),
        value_piece,
        preferred_element_type=jnp.float32,
    )
    running, weight_sum, numerator = (new_max, weight_sum, numerator)
    attended = (
        (numerator / weight_sum[..., None])
        .transpose(1, 0, 2)
        .reshape(tok_rows, head_cols)
        .astype(jnp.bfloat16)
    )
    out_partial = project(lax.all_gather(attended, "row", axis=0, tiled=True), weight=w_out)
    attn_out = to_rows(out_partial, tok_rows)
    resid = stream + attn_out.astype(jnp.float32)
    totals2 = lax.psum(jnp.sum(resid * resid, axis=-1), "col")
    normed2 = (resid * lax.rsqrt(totals2 / D + EPSILON)[:, None] * scale_mlp).astype(jnp.bfloat16)
    section = lax.all_gather(normed2, "row", axis=0, tiled=True)
    gate_up = jnp.concatenate(
        [
            jnp.dot(section, w_gate, preferred_element_type=jnp.float32),
            jnp.dot(section, w_up, preferred_element_type=jnp.float32),
        ],
        axis=1,
    )
    unit_count = w_gate.shape[1]
    share_sum = lax.psum_scatter(
        gate_up.astype(jnp.bfloat16), "col", scatter_dimension=0, tiled=True
    ).astype(jnp.float32)
    part_hidden = (jax.nn.silu(share_sum[:, :unit_count]) * share_sum[:, unit_count:]).astype(
        jnp.bfloat16
    )
    hidden = lax.all_gather(part_hidden, "col", axis=0, tiled=True)
    lowered = lax.psum_scatter(
        jnp.dot(hidden, w_down, preferred_element_type=jnp.float32),
        "row",
        scatter_dimension=0,
        tiled=True,
    )
    return (resid + lowered).astype(jnp.bfloat16)


def gather_rows(block):
    row_count = lax.axis_size("row")
    copies = jnp.broadcast_to(block[None], (row_count,) + block.shape)
    return lax.all_to_all(copies, "row", split_axis=0, concat_axis=0, tiled=True)


def other_core(block):
    return lax.ppermute(block, "col", [(0, 1), (1, 0)])


SQUARE = 4


def spread(block):
    row_count = lax.axis_size("row")
    mine = lax.axis_index("row")
    core = lax.axis_index("col")
    at = lax.rem(mine, SQUARE)
    home = mine // SQUARE == core
    got = []
    for step in range(SQUARE):
        pairs = []
        for chip in range(row_count):
            square, place = chip // SQUARE, chip % SQUARE
            if step > 0:
                pairs.append((2 * chip + square, 2 * (SQUARE * square + (place ^ step)) + square))
            away = 1 - square
            pairs.append((2 * chip + away, 2 * (SQUARE * away + (place ^ step)) + square))
        got.append(lax.ppermute(block, ("row", "col"), pairs))
    got[0] = jnp.where(home, block, got[0])
    stacked = jnp.stack(got)
    order = jnp.arange(SQUARE) ^ at
    return jnp.take(stacked, order, axis=0)


def side_by_side(blocks):
    count, tokens, columns = blocks.shape
    return blocks.transpose(1, 0, 2).reshape(tokens, count * columns)


def few_rows(hidden_states, scale_attn, w_qkv, w_out, scale_mlp, w_gate, w_up, w_down):
    tok_rows, half = hidden_states.shape
    row_count = lax.axis_size("row")
    mine = lax.axis_index("row")
    tokens = tok_rows * row_count
    stream = gather_rows(hidden_states).reshape(tokens, half).astype(jnp.float32)
    squares = jnp.sum(stream * stream, axis=-1, keepdims=True)
    total = squares + other_core(squares)
    inverse = lax.rsqrt(total / D + EPSILON)
    part = project((stream * scale_attn).astype(jnp.bfloat16), w_qkv)
    qkv = ((part + other_core(part.astype(jnp.bfloat16)).astype(jnp.float32)) * inverse).astype(jnp.bfloat16)

    unit = qkv.shape[1] // 3
    first, middle, last = qkv[:, :unit], qkv[:, unit : 2 * unit], qkv[:, 2 * unit :]
    odd = lax.rem(mine, 2) == 1
    kept = jnp.where(odd, last, first)
    sent = jnp.where(odd, first, last)
    from_x = lax.ppermute(middle, "row", [(i, i ^ 1) for i in range(row_count)])
    from_z = lax.ppermute(sent, "row", [(i, i ^ 2) for i in range(row_count)])
    at = lax.rem(mine, SQUARE)
    queries = jnp.where(at == 0, kept, jnp.where(at == 1, from_x, from_z))
    keys = jnp.where((at == 1) | (at == 2), kept, from_x)
    values = jnp.where(at == 3, kept, jnp.where(at == 2, from_x, from_z))

    heads = unit // HS
    queries, keys, values = (v.reshape(tokens, heads, HS) for v in (queries, keys, values))
    scores = jnp.einsum("qhd,khd->hqk", queries, keys, preferred_element_type=jnp.float32) * (1.0 / math.sqrt(HS))
    weights = jnp.exp(scores - jnp.max(scores, axis=-1, keepdims=True))
    mass = jnp.sum(weights, axis=-1, keepdims=True)
    mixed = jnp.einsum("hqk,khd->hqd", weights.astype(jnp.bfloat16), values, preferred_element_type=jnp.float32) / mass
    attended = mixed.transpose(1, 0, 2).reshape(tokens, unit).astype(jnp.bfloat16)

    part = project(side_by_side(spread(attended)), w_out)
    attn_out = (part + other_core(part.astype(jnp.bfloat16)).astype(jnp.float32)).astype(jnp.bfloat16)
    resid = stream + side_by_side(spread(attn_out)).astype(jnp.float32)

    squares = jnp.sum(resid * resid, axis=-1, keepdims=True)
    total = squares + other_core(squares)
    inverse = lax.rsqrt(total / D + EPSILON)
    section = (resid * scale_mlp).astype(jnp.bfloat16)
    gate, upward = project(section, w_gate), project(section, w_up)
    swapped = other_core(jnp.stack([gate, upward]).astype(jnp.bfloat16)).astype(jnp.float32)
    gate = (gate + swapped[0]) * inverse
    upward = (upward + swapped[1]) * inverse
    hidden = (jax.nn.silu(gate) * upward).astype(jnp.bfloat16)
    lowered = project(hidden, w_down).reshape(row_count, tok_rows, half)
    lowered = jnp.sum(lax.all_to_all(lowered, "row", split_axis=0, concat_axis=0, tiled=True), axis=0)
    own = lax.dynamic_slice_in_dim(resid, mine * tok_rows, tok_rows, axis=0)
    return (own + lowered).astype(jnp.bfloat16)


def body(*arrays):
    fits = lax.axis_size("col") == 2 and lax.axis_size("row") == 2 * SQUARE and HEADS % (2 * SQUARE) == 0
    return (few_rows if fits else per_device)(*arrays)


def solution(mesh):
    return jax.shard_map(
        body,
        mesh=mesh,
        in_specs=(
            P(("groups", "row"), "col"),
            P("col"),
            P("col", "row"),
            P("col", "row"),
            P("col"),
            P("col", "row"),
            P("col", "row"),
            P("row", "col"),
        ),
        out_specs=P(("groups", "row"), "col"),
        check_vma=False,
    )
```

```python
import functools
import math

import jax
import jax.numpy as jnp
from jax import lax
from jax.experimental import pallas as pl
from jax.experimental.pallas import tpu as pltpu
from jax.sharding import PartitionSpec as P

HEADS = 48
HS = 128
D = 6144


EPSILON = 1e-06


def project(section, weight):
    return jnp.dot(section, weight, preferred_element_type=jnp.float32)


def to_rows(partial_sum, tok_rows):
    groups = lax.axis_size("col")
    row_count = lax.axis_size("row")
    half_rows = tok_rows // groups
    columns = partial_sum.shape[1]
    ordered = (
        partial_sum.reshape(row_count, groups, half_rows, columns)
        .transpose(1, 0, 2, 3)
        .reshape(-1, columns)
    )
    summed = lax.psum_scatter(ordered.astype(jnp.bfloat16), "col", scatter_dimension=0, tiled=True)
    return lax.all_to_all(
        lax.all_to_all(summed, "row", split_axis=0, concat_axis=1, tiled=True),
        "col",
        split_axis=1,
        concat_axis=0,
        tiled=True,
    )


def per_device(hidden_states, scale_attn, w_qkv, w_out, scale_mlp, w_gate, w_up, w_down):
    tok_rows = hidden_states.shape[0]
    groups = lax.axis_size("col")
    stream = hidden_states.astype(jnp.float32)
    totals = lax.psum(jnp.sum(stream * stream, axis=-1), "col")
    normed = (stream * lax.rsqrt(totals / D + EPSILON)[:, None] * scale_attn).astype(jnp.bfloat16)
    qkv_partial = project(lax.all_gather(normed, "row", axis=0, tiled=True), weight=w_qkv)
    qkv = to_rows(qkv_partial, tok_rows)
    local_heads = HEADS // groups
    head_cols = local_heads * HS
    queries = qkv[:, :head_cols].reshape(tok_rows, local_heads, HS)
    key_rows = qkv[:, head_cols : 2 * head_cols]
    value_rows = qkv[:, 2 * head_cols :]
    factor = 1.0 / math.sqrt(HS)
    running = jnp.full((local_heads, tok_rows), -1e30, jnp.float32)
    key_piece = lax.all_gather(key_rows, "row", axis=0, tiled=True).reshape(-1, local_heads, HS)
    value_piece = lax.all_gather(value_rows, "row", axis=0, tiled=True).reshape(-1, local_heads, HS)
    scores = (
        jnp.einsum("qhd,khd->hqk", queries, key_piece, preferred_element_type=jnp.float32) * factor
    )
    new_max = jnp.maximum(running, jnp.max(scores, axis=-1))
    weights = jnp.exp(scores - new_max[..., None])
    weight_sum = jnp.sum(weights, axis=-1)
    numerator = jnp.einsum(
        "hqk,khd->hqd",
        weights.astype(jnp.bfloat16),
        value_piece,
        preferred_element_type=jnp.float32,
    )
    running, weight_sum, numerator = (new_max, weight_sum, numerator)
    attended = (
        (numerator / weight_sum[..., None])
        .transpose(1, 0, 2)
        .reshape(tok_rows, head_cols)
        .astype(jnp.bfloat16)
    )
    out_partial = project(lax.all_gather(attended, "row", axis=0, tiled=True), weight=w_out)
    attn_out = to_rows(out_partial, tok_rows)
    resid = stream + attn_out.astype(jnp.float32)
    totals2 = lax.psum(jnp.sum(resid * resid, axis=-1), "col")
    normed2 = (resid * lax.rsqrt(totals2 / D + EPSILON)[:, None] * scale_mlp).astype(jnp.bfloat16)
    section = lax.all_gather(normed2, "row", axis=0, tiled=True)
    gate_up = jnp.concatenate(
        [
            jnp.dot(section, w_gate, preferred_element_type=jnp.float32),
            jnp.dot(section, w_up, preferred_element_type=jnp.float32),
        ],
        axis=1,
    )
    unit_count = w_gate.shape[1]
    share_sum = lax.psum_scatter(
        gate_up.astype(jnp.bfloat16), "col", scatter_dimension=0, tiled=True
    ).astype(jnp.float32)
    part_hidden = (jax.nn.silu(share_sum[:, :unit_count]) * share_sum[:, unit_count:]).astype(
        jnp.bfloat16
    )
    hidden = lax.all_gather(part_hidden, "col", axis=0, tiled=True)
    lowered = lax.psum_scatter(
        jnp.dot(hidden, w_down, preferred_element_type=jnp.float32),
        "row",
        scatter_dimension=0,
        tiled=True,
    )
    return (resid + lowered).astype(jnp.bfloat16)


SQUARE = 4
MIB = 2**20


def call(kernel, outs, *arrays, scratch=(), flops=2 * 10**9):
    whole = pl.BlockSpec(memory_space=pltpu.VMEM)
    return pl.pallas_call(
        kernel,
        out_shape=[jax.ShapeDtypeStruct(*out) for out in outs],
        in_specs=[whole] * len(arrays),
        out_specs=[whole] * len(outs),
        scratch_shapes=list(scratch),
        cost_estimate=pl.CostEstimate(flops=flops, bytes_accessed=10**5, transcendentals=0),
        compiler_params=pltpu.CompilerParams(vmem_limit_bytes=2 * MIB),
    )(*arrays)


def other_core(block):
    return lax.ppermute(block, "col", [(0, 1), (1, 0)])


def from_row(block, step):
    count = lax.axis_size("row")
    return lax.ppermute(block, "row", [(i, i ^ step) for i in range(count)])


def spread(block):
    got = []
    for step in range(SQUARE):
        pairs = []
        for chip in range(lax.axis_size("row")):
            square, place = chip // SQUARE, chip % SQUARE
            if step > 0:
                pairs.append((2 * chip + square, 2 * (SQUARE * square + (place ^ step)) + square))
            away = 1 - square
            pairs.append((2 * chip + away, 2 * (SQUARE * away + (place ^ step)) + square))
        got.append(lax.ppermute(block, ("row", "col"), pairs))
    return got


def at_home():
    return lax.axis_index("row") // SQUARE == lax.axis_index("col")


def lanes(values):
    return jnp.broadcast_to(values, (values.shape[0], 128))


def pair_kernel(mine_ref, other_ref, both_ref):
    both_ref[0] = mine_ref[...]
    both_ref[1] = other_ref[...]


def enter_kernel(*refs):
    pairs, (scale_ref, stream_ref, scaled_ref, squares_ref, blocks) = refs[:4], refs[4:]
    mine = lax.axis_index("row")
    for step, pair_ref in enumerate(pairs):
        for near in range(2):
            blocks[mine ^ (2 * step + near)] = pair_ref[near].astype(jnp.float32)
    count, rows, _ = blocks.shape
    for block in range(count):
        stream_ref[rows * block : rows * (block + 1)] = blocks[block]
    stream = stream_ref[...]
    scaled_ref[...] = (stream * scale_ref[...][None, :]).astype(jnp.bfloat16)
    squares_ref[...] = lanes(jnp.sum(stream * stream, axis=-1, keepdims=True))


def product_kernel(columns, left_ref, weight_ref, part_ref, sent_ref):
    for start in range(0, weight_ref.shape[1], columns):
        at = slice(start, start + columns)
        part = jnp.dot(left_ref[...], weight_ref[:, at], preferred_element_type=jnp.float32)
        part_ref[:, at] = part
        sent_ref[:, at] = part.astype(jnp.bfloat16)


def factor(squares_ref, other_ref):
    total = squares_ref[...] + other_ref[...]
    return lax.rsqrt(total[:, :1] / D + EPSILON)


def units_kernel(part_ref, other_ref, squares_ref, squares_other_ref, kept_ref, near_ref, far_ref):
    inverse = factor(squares_ref, squares_other_ref)
    summed = ((part_ref[...] + other_ref[...].astype(jnp.float32)) * inverse).astype(jnp.bfloat16)
    unit = kept_ref.shape[1]
    odd = lax.rem(lax.axis_index("row"), 2) == 1
    first, last = summed[:, :unit], summed[:, 2 * unit :]
    near_ref[...] = summed[:, unit : 2 * unit]

    @pl.when(odd)
    def _():
        kept_ref[...] = last
        far_ref[...] = first

    @pl.when(jnp.logical_not(odd))
    def _():
        kept_ref[...] = first
        far_ref[...] = last


def attend_kernel(kept_ref, near_ref, far_ref, attended_ref, chosen):
    place = lax.rem(lax.axis_index("row"), SQUARE)
    query, key, value = 0, 1, 2
    roles = [(query, key, value), (key, query, value), (key, value, query), (value, key, query)]
    for at in range(SQUARE):

        @pl.when(place == at)
        def _(at=at):
            for role, ref in zip(roles[at], (kept_ref, near_ref, far_ref)):
                chosen[role] = ref[...]

    for start in range(0, kept_ref.shape[1], HS):
        head = slice(start, start + HS)
        scores = lax.dot_general(
            chosen[query, :, head], chosen[key, :, head], (((1,), (1,)), ((), ())), preferred_element_type=jnp.float32
        ) * (1.0 / math.sqrt(HS))
        weights = jnp.exp(scores - jnp.max(scores, axis=-1, keepdims=True))
        mass = jnp.sum(weights, axis=-1, keepdims=True)
        mixed = jnp.dot(weights.astype(jnp.bfloat16), chosen[value, :, head], preferred_element_type=jnp.float32)
        attended_ref[:, head] = (mixed / mass).astype(jnp.bfloat16)


def out_kernel(own_ref, *refs):
    got, (weight_ref, part_ref, sent_ref, blocks) = refs[:SQUARE], refs[SQUARE:]
    unit = own_ref.shape[1]
    place = lax.rem(lax.axis_index("row"), SQUARE)
    blocks[...] = jnp.where(at_home(), own_ref[...], got[0][...])
    part = None
    for step in range(SQUARE):
        left = blocks[...] if step == 0 else got[step][...]
        rows = pl.ds(pl.multiple_of((place ^ step) * unit, 128), unit)
        term = jnp.dot(left, weight_ref[rows, :], preferred_element_type=jnp.float32)
        part = term if part is None else part + term
    part_ref[...] = part
    sent_ref[...] = part.astype(jnp.bfloat16)


def sum_kernel(part_ref, other_ref, summed_ref):
    summed_ref[...] = (part_ref[...] + other_ref[...].astype(jnp.float32)).astype(jnp.bfloat16)


def resid_kernel(own_ref, *refs):
    got, (stream_ref, scale_ref, scaled_ref, squares_ref, tokens_ref, resid, blocks) = refs[:SQUARE], refs[SQUARE:]
    unit = own_ref.shape[1]
    place = lax.rem(lax.axis_index("row"), SQUARE)
    for step in range(SQUARE):
        added = got[step][...]
        if step == 0:
            added = jnp.where(at_home(), own_ref[...], added)
        columns = pl.ds(pl.multiple_of((place ^ step) * unit, 128), unit)
        resid[:, columns] = stream_ref[:, columns] + added.astype(jnp.float32)
    whole = resid[...]
    scaled_ref[...] = (whole * scale_ref[...][None, :]).astype(jnp.bfloat16)
    squares_ref[...] = lanes(jnp.sum(whole * whole, axis=-1, keepdims=True))
    count, rows, _ = blocks.shape
    for block in range(count):
        blocks[block] = whole[rows * block : rows * (block + 1)]
    tokens_ref[...] = blocks[lax.axis_index("row")]


def down_kernel(columns, *refs):
    gate_ref, gate_other_ref, up_ref, up_other_ref, squares_ref, squares_other_ref, weight_ref, blocks_ref, hidden = refs
    inverse = factor(squares_ref, squares_other_ref)
    gate = (gate_ref[...] + gate_other_ref[...].astype(jnp.float32)) * inverse
    upward = (up_ref[...] + up_other_ref[...].astype(jnp.float32)) * inverse
    hidden[...] = (gate / (1.0 + jnp.exp(-gate)) * upward).astype(jnp.bfloat16)
    count, rows, _ = blocks_ref.shape
    for start in range(0, weight_ref.shape[1], columns):
        at = slice(start, start + columns)
        lowered = jnp.dot(hidden[...], weight_ref[:, at], preferred_element_type=jnp.float32)
        for block in range(count):
            blocks_ref[block, :, at] = lowered[rows * block : rows * (block + 1)]


def leave_kernel(tokens_ref, blocks_ref, updated_ref):
    total = tokens_ref[...]
    for block in range(blocks_ref.shape[0]):
        total = total + blocks_ref[block]
    updated_ref[...] = total.astype(jnp.bfloat16)


def few_rows(hidden_states, scale_attn, w_qkv, w_out, scale_mlp, w_gate, w_up, w_down):
    bf16, f32 = jnp.bfloat16, jnp.float32
    tok_rows, half = hidden_states.shape
    count = lax.axis_size("row")
    tokens = tok_rows * count

    [pair] = call(pair_kernel, [((2, tok_rows, half), bf16)], hidden_states, from_row(hidden_states, 1))
    pairs = [pair] + [from_row(pair, 2 * step) for step in range(1, count // 2)]
    stream, scaled, squares = call(
        enter_kernel,
        [((tokens, half), f32), ((tokens, half), bf16), ((tokens, 128), f32)],
        *pairs, scale_attn,
        scratch=[pltpu.VMEM((count, tok_rows, half), f32)],
    )
    squares_other = other_core(squares)
    columns = w_qkv.shape[1]
    part, sent = call(functools.partial(product_kernel, 256), [((tokens, columns), f32), ((tokens, columns), bf16)], scaled, w_qkv)
    unit = columns // 3
    block = ((tokens, unit), bf16)
    kept, near, far = call(units_kernel, [block] * 3, part, other_core(sent), squares, squares_other)
    [attended] = call(
        attend_kernel, [block], kept, from_row(near, 1), from_row(far, 2), scratch=[pltpu.VMEM((3, tokens, unit), bf16)]
    )
    part, sent = call(
        out_kernel,
        [((tokens, unit), f32), block],
        attended, *spread(attended), w_out,
        scratch=[pltpu.VMEM((tokens, unit), bf16)],
    )
    [attn_out] = call(sum_kernel, [block], part, other_core(sent))
    scaled, squares, own = call(
        resid_kernel,
        [((tokens, half), bf16), ((tokens, 128), f32), ((tok_rows, half), f32)],
        attn_out, *spread(attn_out), stream, scale_mlp,
        scratch=[pltpu.VMEM((tokens, half), f32), pltpu.VMEM((count, tok_rows, half), f32)],
    )
    squares_other = other_core(squares)
    units = w_gate.shape[1]
    product = functools.partial(product_kernel, 256)
    parts = [((tokens, units), f32), ((tokens, units), bf16)]
    gate, gate_sent = call(product, parts, scaled, w_gate)
    gate_other = other_core(gate_sent)
    upward, up_sent = call(product, parts, scaled, w_up)
    [lowered] = call(
        functools.partial(down_kernel, 256),
        [((count, tok_rows, half), f32)],
        gate, gate_other, upward, other_core(up_sent), squares, squares_other, w_down,
        scratch=[pltpu.VMEM((tokens, units), bf16)],
    )
    lowered = lax.all_to_all(lowered, "row", split_axis=0, concat_axis=0, tiled=True)
    [updated] = call(leave_kernel, [((tok_rows, half), bf16)], own, lowered)
    return updated


def body(*arrays):
    fits = lax.axis_size("col") == 2 and lax.axis_size("row") == 2 * SQUARE and HEADS % (2 * SQUARE) == 0
    return (few_rows if fits else per_device)(*arrays)


def solution(mesh):
    return jax.shard_map(
        body,
        mesh=mesh,
        in_specs=(
            P(("groups", "row"), "col"),
            P("col"),
            P("col", "row"),
            P("col", "row"),
            P("col"),
            P("col", "row"),
            P("col", "row"),
            P("row", "col"),
        ),
        out_specs=P(("groups", "row"), "col"),
        check_vma=False,
    )
```

```python
import functools
import math

import jax
import jax.numpy as jnp
from jax import lax
from jax.experimental import pallas as pl
from jax.experimental.pallas import tpu as pltpu
from jax.sharding import PartitionSpec as P

HEADS = 48
HS = 128
D = 6144


EPSILON = 1e-06


def project(section, weight):
    return jnp.dot(section, weight, preferred_element_type=jnp.float32)


def to_rows(partial_sum, tok_rows):
    groups = lax.axis_size("col")
    row_count = lax.axis_size("row")
    half_rows = tok_rows // groups
    columns = partial_sum.shape[1]
    ordered = (
        partial_sum.reshape(row_count, groups, half_rows, columns)
        .transpose(1, 0, 2, 3)
        .reshape(-1, columns)
    )
    summed = lax.psum_scatter(ordered.astype(jnp.bfloat16), "col", scatter_dimension=0, tiled=True)
    return lax.all_to_all(
        lax.all_to_all(summed, "row", split_axis=0, concat_axis=1, tiled=True),
        "col",
        split_axis=1,
        concat_axis=0,
        tiled=True,
    )


def per_device(hidden_states, scale_attn, w_qkv, w_out, scale_mlp, w_gate, w_up, w_down):
    tok_rows = hidden_states.shape[0]
    groups = lax.axis_size("col")
    stream = hidden_states.astype(jnp.float32)
    totals = lax.psum(jnp.sum(stream * stream, axis=-1), "col")
    normed = (stream * lax.rsqrt(totals / D + EPSILON)[:, None] * scale_attn).astype(jnp.bfloat16)
    qkv_partial = project(lax.all_gather(normed, "row", axis=0, tiled=True), weight=w_qkv)
    qkv = to_rows(qkv_partial, tok_rows)
    local_heads = HEADS // groups
    head_cols = local_heads * HS
    queries = qkv[:, :head_cols].reshape(tok_rows, local_heads, HS)
    key_rows = qkv[:, head_cols : 2 * head_cols]
    value_rows = qkv[:, 2 * head_cols :]
    factor = 1.0 / math.sqrt(HS)
    running = jnp.full((local_heads, tok_rows), -1e30, jnp.float32)
    key_piece = lax.all_gather(key_rows, "row", axis=0, tiled=True).reshape(-1, local_heads, HS)
    value_piece = lax.all_gather(value_rows, "row", axis=0, tiled=True).reshape(-1, local_heads, HS)
    scores = (
        jnp.einsum("qhd,khd->hqk", queries, key_piece, preferred_element_type=jnp.float32) * factor
    )
    new_max = jnp.maximum(running, jnp.max(scores, axis=-1))
    weights = jnp.exp(scores - new_max[..., None])
    weight_sum = jnp.sum(weights, axis=-1)
    numerator = jnp.einsum(
        "hqk,khd->hqd",
        weights.astype(jnp.bfloat16),
        value_piece,
        preferred_element_type=jnp.float32,
    )
    running, weight_sum, numerator = (new_max, weight_sum, numerator)
    attended = (
        (numerator / weight_sum[..., None])
        .transpose(1, 0, 2)
        .reshape(tok_rows, head_cols)
        .astype(jnp.bfloat16)
    )
    out_partial = project(lax.all_gather(attended, "row", axis=0, tiled=True), weight=w_out)
    attn_out = to_rows(out_partial, tok_rows)
    resid = stream + attn_out.astype(jnp.float32)
    totals2 = lax.psum(jnp.sum(resid * resid, axis=-1), "col")
    normed2 = (resid * lax.rsqrt(totals2 / D + EPSILON)[:, None] * scale_mlp).astype(jnp.bfloat16)
    section = lax.all_gather(normed2, "row", axis=0, tiled=True)
    gate_up = jnp.concatenate(
        [
            jnp.dot(section, w_gate, preferred_element_type=jnp.float32),
            jnp.dot(section, w_up, preferred_element_type=jnp.float32),
        ],
        axis=1,
    )
    unit_count = w_gate.shape[1]
    share_sum = lax.psum_scatter(
        gate_up.astype(jnp.bfloat16), "col", scatter_dimension=0, tiled=True
    ).astype(jnp.float32)
    part_hidden = (jax.nn.silu(share_sum[:, :unit_count]) * share_sum[:, unit_count:]).astype(
        jnp.bfloat16
    )
    hidden = lax.all_gather(part_hidden, "col", axis=0, tiled=True)
    lowered = lax.psum_scatter(
        jnp.dot(hidden, w_down, preferred_element_type=jnp.float32),
        "row",
        scatter_dimension=0,
        tiled=True,
    )
    return (resid + lowered).astype(jnp.bfloat16)


SQUARE = 4
MIB = 2**20


def call(kernel, outs, *arrays, scratch=(), flops=2 * 10**9):
    whole = pl.BlockSpec(memory_space=pltpu.VMEM)
    return pl.pallas_call(
        kernel,
        out_shape=[jax.ShapeDtypeStruct(*out) for out in outs],
        in_specs=[whole] * len(arrays),
        out_specs=[whole] * len(outs),
        scratch_shapes=list(scratch),
        cost_estimate=pl.CostEstimate(flops=flops, bytes_accessed=10**5, transcendentals=0),
        compiler_params=pltpu.CompilerParams(vmem_limit_bytes=3 * MIB),
    )(*arrays)


def other_core(block):
    return lax.ppermute(block, "col", [(0, 1), (1, 0)])


def from_row(block, step):
    count = lax.axis_size("row")
    return lax.ppermute(block, "row", [(i, i ^ step) for i in range(count)])


def spread(block):
    got = []
    for step in range(2):
        pairs = []
        for chip in range(lax.axis_size("row")):
            square = chip // SQUARE
            if step > 0:
                pairs.append((2 * chip + square, 2 * (chip ^ 2) + square))
            pairs.append((2 * chip + 1 - square, 2 * (chip ^ SQUARE ^ (2 * step)) + square))
        got.append(lax.ppermute(block, ("row", "col"), pairs))
    return got


def at_home():
    return lax.axis_index("row") // SQUARE == lax.axis_index("col")


def pair_place():
    return lax.rem(lax.axis_index("row"), SQUARE) // 2


def arrange(own_ref, got):
    return jnp.where(at_home(), own_ref[...], got[0][...]), got[1][...]


def lanes(values):
    return jnp.broadcast_to(values, (values.shape[0], 128))


def bring_kernel(*refs):
    half = len(refs) // 2
    for source, target in zip(refs[:half], refs[half:]):
        target[...] = source[...]


def pair_kernel(mine_ref, other_ref, both_ref):
    both_ref[0] = mine_ref[...]
    both_ref[1] = other_ref[...]


def enter_kernel(*refs):
    pairs, (scale_ref, stream_ref, scaled_ref, squares_ref, blocks) = refs[:4], refs[4:]
    mine = lax.axis_index("row")
    for step, pair_ref in enumerate(pairs):
        for near in range(2):
            blocks[mine ^ (2 * step + near)] = pair_ref[near].astype(jnp.float32)
    count, rows, _ = blocks.shape
    for block in range(count):
        stream_ref[rows * block : rows * (block + 1)] = blocks[block]
    stream = stream_ref[...]
    scaled_ref[...] = (stream * scale_ref[...][None, :]).astype(jnp.bfloat16)
    squares_ref[...] = lanes(jnp.sum(stream * stream, axis=-1, keepdims=True))


def product_kernel(columns, left_ref, weight_ref, part_ref, sent_ref):
    for start in range(0, weight_ref.shape[1], columns):
        at = slice(start, start + columns)
        part = jnp.dot(left_ref[...], weight_ref[:, at], preferred_element_type=jnp.float32)
        part_ref[:, at] = part
        sent_ref[:, at] = part.astype(jnp.bfloat16)


def factor(squares_ref, other_ref):
    total = squares_ref[...] + other_ref[...]
    return lax.rsqrt(total[:, :1] / D + EPSILON)


def units_kernel(part_ref, other_ref, squares_ref, squares_other_ref, near_ref, far_ref):
    inverse = factor(squares_ref, squares_other_ref)
    summed = ((part_ref[...] + other_ref[...].astype(jnp.float32)) * inverse).astype(jnp.bfloat16)
    unit = far_ref.shape[1]
    odd = lax.rem(lax.axis_index("row"), 2) == 1

    @pl.when(odd)
    def _():
        near_ref[...] = summed[:, unit:]
        far_ref[...] = summed[:, :unit]

    @pl.when(jnp.logical_not(odd))
    def _():
        near_ref[...] = summed[:, : 2 * unit]
        far_ref[...] = summed[:, 2 * unit :]


def attend_kernel(kept_ref, near_ref, straight_ref, across_ref, attended_ref, chosen):
    place = lax.rem(lax.axis_index("row"), SQUARE)
    unit = straight_ref.shape[1]
    query, key, value = 0, 1, 2
    roles = [(query, key, value), (key, query, value), (key, value, query), (value, key, query)]
    for at in range(SQUARE):

        @pl.when(place == at)
        def _(at=at):
            kept, near, far = roles[at]
            chosen[kept] = kept_ref[...]
            chosen[near] = near_ref[...]
            first, last = (straight_ref, across_ref) if at % 2 == 0 else (across_ref, straight_ref)
            chosen[far, :, :unit] = first[...]
            chosen[far, :, unit:] = last[...]

    for start in range(0, kept_ref.shape[1], HS):
        head = slice(start, start + HS)
        scores = lax.dot_general(
            chosen[query, :, head], chosen[key, :, head], (((1,), (1,)), ((), ())), preferred_element_type=jnp.float32
        ) * (1.0 / math.sqrt(HS))
        weights = jnp.exp(scores - jnp.max(scores, axis=-1, keepdims=True))
        mass = jnp.sum(weights, axis=-1, keepdims=True)
        mixed = jnp.dot(weights.astype(jnp.bfloat16), chosen[value, :, head], preferred_element_type=jnp.float32)
        attended_ref[:, head] = (mixed / mass).astype(jnp.bfloat16)


def out_kernel(own_ref, *refs):
    got, (weight_ref, part_ref) = refs[:2], refs[2:]
    width = own_ref.shape[1]
    part = None
    for step, left in enumerate(arrange(own_ref, got)):
        rows = pl.ds(pl.multiple_of((pair_place() ^ step) * width, 128), width)
        term = jnp.dot(left, weight_ref[rows, :], preferred_element_type=jnp.float32)
        part = term if part is None else part + term
    part_ref[...] = part.astype(jnp.bfloat16)


def join_kernel(part_ref, core_ref, beside_ref, beside_core_ref, joined_ref):
    width = part_ref.shape[1]
    own = (part_ref[...].astype(jnp.float32) + core_ref[...].astype(jnp.float32)).astype(jnp.bfloat16)
    beside = (beside_ref[...].astype(jnp.float32) + beside_core_ref[...].astype(jnp.float32)).astype(jnp.bfloat16)
    odd = lax.rem(lax.axis_index("row"), 2) == 1
    joined_ref[:, :width] = jnp.where(odd, beside, own)
    joined_ref[:, width:] = jnp.where(odd, own, beside)


def resid_kernel(own_ref, *refs):
    got, (stream_ref, scale_ref, scaled_ref, squares_ref, tokens_ref, resid, blocks) = refs[:2], refs[2:]
    width = own_ref.shape[1]
    for step, added in enumerate(arrange(own_ref, got)):
        columns = pl.ds(pl.multiple_of((pair_place() ^ step) * width, 128), width)
        resid[:, columns] = stream_ref[:, columns] + added.astype(jnp.float32)
    whole = resid[...]
    scaled_ref[...] = (whole * scale_ref[...][None, :]).astype(jnp.bfloat16)
    squares_ref[...] = lanes(jnp.sum(whole * whole, axis=-1, keepdims=True))
    count, rows, _ = blocks.shape
    for block in range(count):
        blocks[block] = whole[rows * block : rows * (block + 1)]
    tokens_ref[...] = blocks[lax.axis_index("row")]


def down_kernel(columns, *refs):
    gate_ref, gate_other_ref, up_ref, up_other_ref, squares_ref, squares_other_ref, weight_ref, blocks_ref, hidden = refs
    inverse = factor(squares_ref, squares_other_ref)
    gate = (gate_ref[...] + gate_other_ref[...].astype(jnp.float32)) * inverse
    upward = (up_ref[...] + up_other_ref[...].astype(jnp.float32)) * inverse
    hidden[...] = (gate / (1.0 + jnp.exp(-gate)) * upward).astype(jnp.bfloat16)
    count, rows, _ = blocks_ref.shape
    for start in range(0, weight_ref.shape[1], columns):
        at = slice(start, start + columns)
        lowered = jnp.dot(hidden[...], weight_ref[:, at], preferred_element_type=jnp.float32)
        for block in range(count):
            blocks_ref[block, :, at] = lowered[rows * block : rows * (block + 1)].astype(jnp.bfloat16)


def leave_kernel(tokens_ref, blocks_ref, updated_ref):
    total = tokens_ref[...]
    for block in range(blocks_ref.shape[0]):
        total = total + blocks_ref[block].astype(jnp.float32)
    updated_ref[...] = total.astype(jnp.bfloat16)


def few_rows(hidden_states, scale_attn, w_qkv, w_out, scale_mlp, w_gate, w_up, w_down):
    bf16, f32 = jnp.bfloat16, jnp.float32
    tok_rows, half = hidden_states.shape
    count = lax.axis_size("row")
    tokens = tok_rows * count

    beside = from_row(hidden_states, 1)
    held = (hidden_states, scale_attn)
    own, scale_attn = call(bring_kernel, [(v.shape, v.dtype) for v in held], *held)
    [pair] = call(pair_kernel, [((2, tok_rows, half), bf16)], own, beside)
    pairs = [pair] + [from_row(pair, 2 * step) for step in range(1, count // 2)]
    stream, scaled, squares = call(
        enter_kernel,
        [((tokens, half), f32), ((tokens, half), bf16), ((tokens, 128), f32)],
        *pairs, scale_attn,
        scratch=[pltpu.VMEM((count, tok_rows, half), f32)],
    )
    squares_other = other_core(squares)
    columns = w_qkv.shape[1]
    part, sent = call(functools.partial(product_kernel, 256), [((tokens, columns), f32), ((tokens, columns), bf16)], scaled, w_qkv)
    unit = columns // 3
    block, double = ((tokens, unit), bf16), ((tokens, 2 * unit), bf16)
    near, far = call(units_kernel, [double, block], part, other_core(sent), squares, squares_other)
    [attended] = call(
        attend_kernel, [double], near, from_row(near, 1), from_row(far, 2), from_row(far, 3),
        scratch=[pltpu.VMEM((3, tokens, 2 * unit), bf16)],
    )
    [part] = call(out_kernel, [block], attended, *spread(attended), w_out)
    across = lax.ppermute(part, ("row", "col"), [(i, i ^ 3) for i in range(2 * count)])
    [joined] = call(join_kernel, [double], part, other_core(part), from_row(part, 1), across)
    scaled, squares, own = call(
        resid_kernel,
        [((tokens, half), bf16), ((tokens, 128), f32), ((tok_rows, half), f32)],
        joined, *spread(joined), stream, scale_mlp,
        scratch=[pltpu.VMEM((tokens, half), f32), pltpu.VMEM((count, tok_rows, half), f32)],
    )
    squares_other = other_core(squares)
    units = w_gate.shape[1]
    product = functools.partial(product_kernel, 256)
    parts = [((tokens, units), f32), ((tokens, units), bf16)]
    gate, gate_sent = call(product, parts, scaled, w_gate)
    gate_other = other_core(gate_sent)
    upward, up_sent = call(product, parts, scaled, w_up)
    [lowered] = call(
        functools.partial(down_kernel, 256),
        [((count, tok_rows, half), bf16)],
        gate, gate_other, upward, other_core(up_sent), squares, squares_other, w_down,
        scratch=[pltpu.VMEM((tokens, units), bf16)],
    )
    lowered = lax.all_to_all(lowered, "row", split_axis=0, concat_axis=0, tiled=True)
    [updated] = call(leave_kernel, [((tok_rows, half), bf16)], own, lowered)
    return updated


def body(*arrays):
    fits = lax.axis_size("col") == 2 and lax.axis_size("row") == 2 * SQUARE and HEADS % (2 * SQUARE) == 0
    return (few_rows if fits else per_device)(*arrays)


def solution(mesh):
    return jax.shard_map(
        body,
        mesh=mesh,
        in_specs=(
            P(("groups", "row"), "col"),
            P("col"),
            P("col", "row"),
            P("col", "row"),
            P("col"),
            P("col", "row"),
            P("col", "row"),
            P("row", "col"),
        ),
        out_specs=P(("groups", "row"), "col"),
        check_vma=False,
    )
```

```python
import functools
import math

import jax
import jax.numpy as jnp
from jax import lax
from jax.experimental import pallas as pl
from jax.experimental.pallas import tpu as pltpu
from jax.sharding import PartitionSpec as P

HEADS = 48
HS = 128
D = 6144


EPSILON = 1e-06


def project(section, weight):
    return jnp.dot(section, weight, preferred_element_type=jnp.float32)


def to_rows(partial_sum, tok_rows):
    groups = lax.axis_size("col")
    row_count = lax.axis_size("row")
    half_rows = tok_rows // groups
    columns = partial_sum.shape[1]
    ordered = (
        partial_sum.reshape(row_count, groups, half_rows, columns)
        .transpose(1, 0, 2, 3)
        .reshape(-1, columns)
    )
    summed = lax.psum_scatter(ordered.astype(jnp.bfloat16), "col", scatter_dimension=0, tiled=True)
    return lax.all_to_all(
        lax.all_to_all(summed, "row", split_axis=0, concat_axis=1, tiled=True),
        "col",
        split_axis=1,
        concat_axis=0,
        tiled=True,
    )


def per_device(hidden_states, scale_attn, w_qkv, w_out, scale_mlp, w_gate, w_up, w_down):
    tok_rows = hidden_states.shape[0]
    groups = lax.axis_size("col")
    stream = hidden_states.astype(jnp.float32)
    totals = lax.psum(jnp.sum(stream * stream, axis=-1), "col")
    normed = (stream * lax.rsqrt(totals / D + EPSILON)[:, None] * scale_attn).astype(jnp.bfloat16)
    qkv_partial = project(lax.all_gather(normed, "row", axis=0, tiled=True), weight=w_qkv)
    qkv = to_rows(qkv_partial, tok_rows)
    local_heads = HEADS // groups
    head_cols = local_heads * HS
    queries = qkv[:, :head_cols].reshape(tok_rows, local_heads, HS)
    key_rows = qkv[:, head_cols : 2 * head_cols]
    value_rows = qkv[:, 2 * head_cols :]
    factor = 1.0 / math.sqrt(HS)
    running = jnp.full((local_heads, tok_rows), -1e30, jnp.float32)
    key_piece = lax.all_gather(key_rows, "row", axis=0, tiled=True).reshape(-1, local_heads, HS)
    value_piece = lax.all_gather(value_rows, "row", axis=0, tiled=True).reshape(-1, local_heads, HS)
    scores = (
        jnp.einsum("qhd,khd->hqk", queries, key_piece, preferred_element_type=jnp.float32) * factor
    )
    new_max = jnp.maximum(running, jnp.max(scores, axis=-1))
    weights = jnp.exp(scores - new_max[..., None])
    weight_sum = jnp.sum(weights, axis=-1)
    numerator = jnp.einsum(
        "hqk,khd->hqd",
        weights.astype(jnp.bfloat16),
        value_piece,
        preferred_element_type=jnp.float32,
    )
    running, weight_sum, numerator = (new_max, weight_sum, numerator)
    attended = (
        (numerator / weight_sum[..., None])
        .transpose(1, 0, 2)
        .reshape(tok_rows, head_cols)
        .astype(jnp.bfloat16)
    )
    out_partial = project(lax.all_gather(attended, "row", axis=0, tiled=True), weight=w_out)
    attn_out = to_rows(out_partial, tok_rows)
    resid = stream + attn_out.astype(jnp.float32)
    totals2 = lax.psum(jnp.sum(resid * resid, axis=-1), "col")
    normed2 = (resid * lax.rsqrt(totals2 / D + EPSILON)[:, None] * scale_mlp).astype(jnp.bfloat16)
    section = lax.all_gather(normed2, "row", axis=0, tiled=True)
    gate_up = jnp.concatenate(
        [
            jnp.dot(section, w_gate, preferred_element_type=jnp.float32),
            jnp.dot(section, w_up, preferred_element_type=jnp.float32),
        ],
        axis=1,
    )
    unit_count = w_gate.shape[1]
    share_sum = lax.psum_scatter(
        gate_up.astype(jnp.bfloat16), "col", scatter_dimension=0, tiled=True
    ).astype(jnp.float32)
    part_hidden = (jax.nn.silu(share_sum[:, :unit_count]) * share_sum[:, unit_count:]).astype(
        jnp.bfloat16
    )
    hidden = lax.all_gather(part_hidden, "col", axis=0, tiled=True)
    lowered = lax.psum_scatter(
        jnp.dot(hidden, w_down, preferred_element_type=jnp.float32),
        "row",
        scatter_dimension=0,
        tiled=True,
    )
    return (resid + lowered).astype(jnp.bfloat16)


SQUARE = 4
MIB = 2**20


def call(kernel, outs, *arrays, scratch=(), flops=2 * 10**9):
    whole = pl.BlockSpec(memory_space=pltpu.VMEM)
    return pl.pallas_call(
        kernel,
        out_shape=[jax.ShapeDtypeStruct(*out) for out in outs],
        in_specs=[whole] * len(arrays),
        out_specs=[whole] * len(outs),
        scratch_shapes=list(scratch),
        cost_estimate=pl.CostEstimate(flops=flops, bytes_accessed=10**5, transcendentals=0),
        compiler_params=pltpu.CompilerParams(vmem_limit_bytes=3 * MIB),
    )(*arrays)


def other_core(block):
    return lax.ppermute(block, "col", [(0, 1), (1, 0)])


def from_row(block, step):
    count = lax.axis_size("row")
    return lax.ppermute(block, "row", [(i, i ^ step) for i in range(count)])


def spread(block):
    got = []
    for step in range(2):
        pairs = []
        for chip in range(lax.axis_size("row")):
            square = chip // SQUARE
            if step > 0:
                pairs.append((2 * chip + square, 2 * (chip ^ 2) + square))
            pairs.append((2 * chip + 1 - square, 2 * (chip ^ SQUARE ^ (2 * step)) + square))
        got.append(lax.ppermute(block, ("row", "col"), pairs))
    return got


def at_home():
    return lax.axis_index("row") // SQUARE == lax.axis_index("col")


def pair_place():
    return lax.rem(lax.axis_index("row"), SQUARE) // 2


def arrange(own_ref, got):
    return jnp.where(at_home(), own_ref[...], got[0][...]), got[1][...]


def lanes(values):
    return jnp.broadcast_to(values, (values.shape[0], 128))


def bring_kernel(*refs):
    half = len(refs) // 2
    for source, target in zip(refs[:half], refs[half:]):
        target[...] = source[...]


def pair_kernel(mine_ref, other_ref, both_ref):
    both_ref[0] = mine_ref[...]
    both_ref[1] = other_ref[...]


def enter_kernel(*refs):
    pairs, (scale_ref, stream_ref, scaled_ref, squares_ref, blocks) = refs[:4], refs[4:]
    mine = lax.axis_index("row")
    for step, pair_ref in enumerate(pairs):
        for near in range(2):
            blocks[mine ^ (2 * step + near)] = pair_ref[near].astype(jnp.float32)
    count, rows, _ = blocks.shape
    for block in range(count):
        stream_ref[rows * block : rows * (block + 1)] = blocks[block]
    stream = stream_ref[...]
    scaled_ref[...] = (stream * scale_ref[...][None, :]).astype(jnp.bfloat16)
    squares_ref[...] = lanes(jnp.sum(stream * stream, axis=-1, keepdims=True))


def product_kernel(columns, left_ref, weight_ref, part_ref, sent_ref):
    for start in range(0, weight_ref.shape[1], columns):
        at = slice(start, start + columns)
        part = jnp.dot(left_ref[...], weight_ref[:, at], preferred_element_type=jnp.float32)
        part_ref[:, at] = part
        sent_ref[:, at] = part.astype(jnp.bfloat16)


def factor(squares_ref, other_ref):
    total = squares_ref[...] + other_ref[...]
    return lax.rsqrt(total[:, :1] / D + EPSILON)


def units_kernel(part_ref, other_ref, squares_ref, squares_other_ref, near_ref, far_ref):
    inverse = factor(squares_ref, squares_other_ref)
    summed = ((part_ref[...] + other_ref[...].astype(jnp.float32)) * inverse).astype(jnp.bfloat16)
    unit = far_ref.shape[1]
    odd = lax.rem(lax.axis_index("row"), 2) == 1

    @pl.when(odd)
    def _():
        near_ref[...] = summed[:, unit:]
        far_ref[...] = summed[:, :unit]

    @pl.when(jnp.logical_not(odd))
    def _():
        near_ref[...] = summed[:, : 2 * unit]
        far_ref[...] = summed[:, 2 * unit :]


def attend_kernel(kept_ref, near_ref, straight_ref, across_ref, attended_ref, chosen):
    place = lax.rem(lax.axis_index("row"), SQUARE)
    unit = straight_ref.shape[1]
    query, key, value = 0, 1, 2
    roles = [(query, key, value), (key, query, value), (key, value, query), (value, key, query)]
    for at in range(SQUARE):

        @pl.when(place == at)
        def _(at=at):
            kept, near, far = roles[at]
            chosen[kept] = kept_ref[...]
            chosen[near] = near_ref[...]
            first, last = (straight_ref, across_ref) if at % 2 == 0 else (across_ref, straight_ref)
            chosen[far, :, :unit] = first[...]
            chosen[far, :, unit:] = last[...]

    for start in range(0, kept_ref.shape[1], HS):
        head = slice(start, start + HS)
        scores = lax.dot_general(
            chosen[query, :, head], chosen[key, :, head], (((1,), (1,)), ((), ())), preferred_element_type=jnp.float32
        ) * (1.0 / math.sqrt(HS))
        weights = jnp.exp(scores - jnp.max(scores, axis=-1, keepdims=True))
        mass = jnp.sum(weights, axis=-1, keepdims=True)
        mixed = jnp.dot(weights.astype(jnp.bfloat16), chosen[value, :, head], preferred_element_type=jnp.float32)
        attended_ref[:, head] = (mixed / mass).astype(jnp.bfloat16)


def out_kernel(own_ref, *refs):
    got, (weight_ref, part_ref) = refs[:2], refs[2:]
    width = own_ref.shape[1]
    part = None
    for step, left in enumerate(arrange(own_ref, got)):
        rows = pl.ds(pl.multiple_of((pair_place() ^ step) * width, 128), width)
        term = jnp.dot(left, weight_ref[rows, :], preferred_element_type=jnp.float32)
        part = term if part is None else part + term
    part_ref[...] = part.astype(jnp.bfloat16)


def join_kernel(part_ref, core_ref, beside_ref, beside_core_ref, joined_ref):
    width = part_ref.shape[1]
    own = (part_ref[...].astype(jnp.float32) + core_ref[...].astype(jnp.float32)).astype(jnp.bfloat16)
    beside = (beside_ref[...].astype(jnp.float32) + beside_core_ref[...].astype(jnp.float32)).astype(jnp.bfloat16)
    odd = lax.rem(lax.axis_index("row"), 2) == 1
    joined_ref[:, :width] = jnp.where(odd, beside, own)
    joined_ref[:, width:] = jnp.where(odd, own, beside)


def resid_kernel(own_ref, *refs):
    got, (stream_ref, scale_ref, scaled_ref, squares_ref, tokens_ref, resid, blocks) = refs[:2], refs[2:]
    width = own_ref.shape[1]
    for step, added in enumerate(arrange(own_ref, got)):
        columns = pl.ds(pl.multiple_of((pair_place() ^ step) * width, 128), width)
        resid[:, columns] = stream_ref[:, columns] + added.astype(jnp.float32)
    whole = resid[...]
    scaled_ref[...] = (whole * scale_ref[...][None, :]).astype(jnp.bfloat16)
    squares_ref[...] = lanes(jnp.sum(whole * whole, axis=-1, keepdims=True))
    count, rows, _ = blocks.shape
    for block in range(count):
        blocks[block] = whole[rows * block : rows * (block + 1)]
    tokens_ref[...] = blocks[lax.axis_index("row")]


def down_kernel(columns, *refs):
    gate_ref, gate_other_ref, up_ref, up_other_ref, squares_ref, squares_other_ref, weight_ref, blocks_ref, hidden = refs
    inverse = factor(squares_ref, squares_other_ref)
    gate = (gate_ref[...] + gate_other_ref[...].astype(jnp.float32)) * inverse
    upward = (up_ref[...] + up_other_ref[...].astype(jnp.float32)) * inverse
    hidden[...] = (gate / (1.0 + jnp.exp(-gate)) * upward).astype(jnp.bfloat16)
    count, rows, _ = blocks_ref.shape
    for start in range(0, weight_ref.shape[1], columns):
        at = slice(start, start + columns)
        lowered = jnp.dot(hidden[...], weight_ref[:, at], preferred_element_type=jnp.float32)
        for block in range(count):
            blocks_ref[block, :, at] = lowered[rows * block : rows * (block + 1)].astype(jnp.bfloat16)


def leave_kernel(tokens_ref, blocks_ref, updated_ref):
    total = tokens_ref[...]
    for block in range(blocks_ref.shape[0]):
        total = total + blocks_ref[block].astype(jnp.float32)
    updated_ref[...] = total.astype(jnp.bfloat16)


def few_rows(hidden_states, scale_attn, w_qkv, w_out, scale_mlp, w_gate, w_up, w_down):
    bf16, f32 = jnp.bfloat16, jnp.float32
    tok_rows, half = hidden_states.shape
    count = lax.axis_size("row")
    tokens = tok_rows * count

    beside = from_row(hidden_states, 1)
    held = (hidden_states, scale_attn)
    own, scale_attn = call(bring_kernel, [(v.shape, v.dtype) for v in held], *held)
    [pair] = call(pair_kernel, [((2, tok_rows, half), bf16)], own, beside)
    pairs = [pair] + [from_row(pair, 2 * step) for step in range(1, count // 2)]
    stream, scaled, squares = call(
        enter_kernel,
        [((tokens, half), f32), ((tokens, half), bf16), ((tokens, 128), f32)],
        *pairs, scale_attn,
        scratch=[pltpu.VMEM((count, tok_rows, half), f32)],
    )
    squares_other = other_core(squares)
    columns = w_qkv.shape[1]
    part, sent = call(functools.partial(product_kernel, 256), [((tokens, columns), f32), ((tokens, columns), bf16)], scaled, w_qkv)
    unit = columns // 3
    block, double = ((tokens, unit), bf16), ((tokens, 2 * unit), bf16)
    near, far = call(units_kernel, [double, block], part, other_core(sent), squares, squares_other)
    [attended] = call(
        attend_kernel, [double], near, from_row(near, 1), from_row(far, 2), from_row(far, 3),
        scratch=[pltpu.VMEM((3, tokens, 2 * unit), bf16)],
    )
    [part] = call(out_kernel, [block], attended, *spread(attended), w_out)
    across = lax.ppermute(part, ("row", "col"), [(i, i ^ 3) for i in range(2 * count)])
    [joined] = call(join_kernel, [double], part, other_core(part), from_row(part, 1), across, flops=10 * 10**8)
    scaled, squares, own = call(
        resid_kernel,
        [((tokens, half), bf16), ((tokens, 128), f32), ((tok_rows, half), f32)],
        joined, *spread(joined), stream, scale_mlp,
        flops=5 * 10**8,
        scratch=[pltpu.VMEM((tokens, half), f32), pltpu.VMEM((count, tok_rows, half), f32)],
    )
    squares_other = other_core(squares)
    units = w_gate.shape[1]
    product = functools.partial(product_kernel, 256)
    parts = [((tokens, units), f32), ((tokens, units), bf16)]
    gate, gate_sent = call(product, parts, scaled, w_gate)
    gate_other = other_core(gate_sent)
    upward, up_sent = call(product, parts, scaled, w_up)
    [lowered] = call(
        functools.partial(down_kernel, 256),
        [((count, tok_rows, half), bf16)],
        gate, gate_other, upward, other_core(up_sent), squares, squares_other, w_down,
        scratch=[pltpu.VMEM((tokens, units), bf16)],
    )
    lowered = lax.all_to_all(lowered, "row", split_axis=0, concat_axis=0, tiled=True)
    [updated] = call(leave_kernel, [((tok_rows, half), bf16)], own, lowered)
    return updated


def body(*arrays):
    fits = lax.axis_size("col") == 2 and lax.axis_size("row") == 2 * SQUARE and HEADS % (2 * SQUARE) == 0
    return (few_rows if fits else per_device)(*arrays)


def solution(mesh):
    return jax.shard_map(
        body,
        mesh=mesh,
        in_specs=(
            P(("groups", "row"), "col"),
            P("col"),
            P("col", "row"),
            P("col", "row"),
            P("col"),
            P("col", "row"),
            P("col", "row"),
            P("row", "col"),
        ),
        out_specs=P(("groups", "row"), "col"),
        check_vma=False,
    )
```

```python
import functools
import math

import jax
import jax.numpy as jnp
from jax import lax
from jax.experimental import pallas as pl
from jax.experimental.pallas import tpu as pltpu
from jax.sharding import PartitionSpec as P

HEADS = 48
HS = 128
D = 6144


EPSILON = 1e-06


def project(section, weight):
    return jnp.dot(section, weight, preferred_element_type=jnp.float32)


def to_rows(partial_sum, tok_rows):
    groups = lax.axis_size("col")
    row_count = lax.axis_size("row")
    half_rows = tok_rows // groups
    columns = partial_sum.shape[1]
    ordered = (
        partial_sum.reshape(row_count, groups, half_rows, columns)
        .transpose(1, 0, 2, 3)
        .reshape(-1, columns)
    )
    summed = lax.psum_scatter(ordered.astype(jnp.bfloat16), "col", scatter_dimension=0, tiled=True)
    return lax.all_to_all(
        lax.all_to_all(summed, "row", split_axis=0, concat_axis=1, tiled=True),
        "col",
        split_axis=1,
        concat_axis=0,
        tiled=True,
    )


def per_device(hidden_states, scale_attn, w_qkv, w_out, scale_mlp, w_gate, w_up, w_down):
    tok_rows = hidden_states.shape[0]
    groups = lax.axis_size("col")
    stream = hidden_states.astype(jnp.float32)
    totals = lax.psum(jnp.sum(stream * stream, axis=-1), "col")
    normed = (stream * lax.rsqrt(totals / D + EPSILON)[:, None] * scale_attn).astype(jnp.bfloat16)
    qkv_partial = project(lax.all_gather(normed, "row", axis=0, tiled=True), weight=w_qkv)
    qkv = to_rows(qkv_partial, tok_rows)
    local_heads = HEADS // groups
    head_cols = local_heads * HS
    queries = qkv[:, :head_cols].reshape(tok_rows, local_heads, HS)
    key_rows = qkv[:, head_cols : 2 * head_cols]
    value_rows = qkv[:, 2 * head_cols :]
    factor = 1.0 / math.sqrt(HS)
    running = jnp.full((local_heads, tok_rows), -1e30, jnp.float32)
    key_piece = lax.all_gather(key_rows, "row", axis=0, tiled=True).reshape(-1, local_heads, HS)
    value_piece = lax.all_gather(value_rows, "row", axis=0, tiled=True).reshape(-1, local_heads, HS)
    scores = (
        jnp.einsum("qhd,khd->hqk", queries, key_piece, preferred_element_type=jnp.float32) * factor
    )
    new_max = jnp.maximum(running, jnp.max(scores, axis=-1))
    weights = jnp.exp(scores - new_max[..., None])
    weight_sum = jnp.sum(weights, axis=-1)
    numerator = jnp.einsum(
        "hqk,khd->hqd",
        weights.astype(jnp.bfloat16),
        value_piece,
        preferred_element_type=jnp.float32,
    )
    running, weight_sum, numerator = (new_max, weight_sum, numerator)
    attended = (
        (numerator / weight_sum[..., None])
        .transpose(1, 0, 2)
        .reshape(tok_rows, head_cols)
        .astype(jnp.bfloat16)
    )
    out_partial = project(lax.all_gather(attended, "row", axis=0, tiled=True), weight=w_out)
    attn_out = to_rows(out_partial, tok_rows)
    resid = stream + attn_out.astype(jnp.float32)
    totals2 = lax.psum(jnp.sum(resid * resid, axis=-1), "col")
    normed2 = (resid * lax.rsqrt(totals2 / D + EPSILON)[:, None] * scale_mlp).astype(jnp.bfloat16)
    section = lax.all_gather(normed2, "row", axis=0, tiled=True)
    gate_up = jnp.concatenate(
        [
            jnp.dot(section, w_gate, preferred_element_type=jnp.float32),
            jnp.dot(section, w_up, preferred_element_type=jnp.float32),
        ],
        axis=1,
    )
    unit_count = w_gate.shape[1]
    share_sum = lax.psum_scatter(
        gate_up.astype(jnp.bfloat16), "col", scatter_dimension=0, tiled=True
    ).astype(jnp.float32)
    part_hidden = (jax.nn.silu(share_sum[:, :unit_count]) * share_sum[:, unit_count:]).astype(
        jnp.bfloat16
    )
    hidden = lax.all_gather(part_hidden, "col", axis=0, tiled=True)
    lowered = lax.psum_scatter(
        jnp.dot(hidden, w_down, preferred_element_type=jnp.float32),
        "row",
        scatter_dimension=0,
        tiled=True,
    )
    return (resid + lowered).astype(jnp.bfloat16)


SQUARE = 4
MIB = 2**20


def call(kernel, outs, *arrays, scratch=(), flops=2 * 10**9):
    whole = pl.BlockSpec(memory_space=pltpu.VMEM)
    return pl.pallas_call(
        kernel,
        out_shape=[jax.ShapeDtypeStruct(*out) for out in outs],
        in_specs=[whole] * len(arrays),
        out_specs=[whole] * len(outs),
        scratch_shapes=list(scratch),
        cost_estimate=pl.CostEstimate(flops=flops, bytes_accessed=10**5, transcendentals=0),
        compiler_params=pltpu.CompilerParams(vmem_limit_bytes=3 * MIB),
    )(*arrays)


def other_core(block):
    return lax.ppermute(block, "col", [(0, 1), (1, 0)])


def from_row(block, step):
    count = lax.axis_size("row")
    return lax.ppermute(block, "row", [(i, i ^ step) for i in range(count)])


def spread(block):
    got = []
    for step in range(2):
        pairs = []
        for chip in range(lax.axis_size("row")):
            square = chip // SQUARE
            if step > 0:
                pairs.append((2 * chip + square, 2 * (chip ^ 2) + square))
            pairs.append((2 * chip + 1 - square, 2 * (chip ^ SQUARE ^ (2 * step)) + square))
        got.append(lax.ppermute(block, ("row", "col"), pairs))
    return got


def at_home():
    return lax.axis_index("row") // SQUARE == lax.axis_index("col")


def pair_place():
    return lax.rem(lax.axis_index("row"), SQUARE) // 2


def arrange(own_ref, got):
    return jnp.where(at_home(), own_ref[...], got[0][...]), got[1][...]


def lanes(values):
    return jnp.broadcast_to(values, (values.shape[0], 128))


def bring_kernel(*refs):
    half = len(refs) // 2
    for source, target in zip(refs[:half], refs[half:]):
        target[...] = source[...]


def scale_kernel(scale_ref, _, brought_ref):
    brought_ref[...] = scale_ref[...]


def pair_kernel(*refs):
    for place, ref in enumerate(refs[:-1]):
        refs[-1][place] = ref[...]


def enter_kernel(*refs):
    columns, (scale_ref, stream_ref, scaled_ref, squares_ref, blocks) = refs[:2], refs[2:]
    mine = lax.axis_index("row")
    for near, column_ref in enumerate(columns):
        for step in range(column_ref.shape[0]):
            blocks[mine ^ (2 * step + near)] = column_ref[step].astype(jnp.float32)
    count, rows, _ = blocks.shape
    for block in range(count):
        stream_ref[rows * block : rows * (block + 1)] = blocks[block]
    stream = stream_ref[...]
    scaled_ref[...] = (stream * scale_ref[...][None, :]).astype(jnp.bfloat16)
    squares_ref[...] = lanes(jnp.sum(stream * stream, axis=-1, keepdims=True))


def product_kernel(columns, left_ref, weight_ref, part_ref, sent_ref):
    for start in range(0, weight_ref.shape[1], columns):
        at = slice(start, start + columns)
        part = jnp.dot(left_ref[...], weight_ref[:, at], preferred_element_type=jnp.float32)
        part_ref[:, at] = part
        sent_ref[:, at] = part.astype(jnp.bfloat16)


def factor(squares_ref, other_ref):
    total = squares_ref[...] + other_ref[...]
    return lax.rsqrt(total[:, :1] / D + EPSILON)


def units_kernel(part_ref, other_ref, squares_ref, squares_other_ref, near_ref, far_ref):
    inverse = factor(squares_ref, squares_other_ref)
    summed = ((part_ref[...] + other_ref[...].astype(jnp.float32)) * inverse).astype(jnp.bfloat16)
    unit = far_ref.shape[1]
    odd = lax.rem(lax.axis_index("row"), 2) == 1

    @pl.when(odd)
    def _():
        near_ref[...] = summed[:, unit:]
        far_ref[...] = summed[:, :unit]

    @pl.when(jnp.logical_not(odd))
    def _():
        near_ref[...] = summed[:, : 2 * unit]
        far_ref[...] = summed[:, 2 * unit :]


def attend_kernel(kept_ref, near_ref, straight_ref, across_ref, attended_ref, chosen):
    place = lax.rem(lax.axis_index("row"), SQUARE)
    unit = straight_ref.shape[1]
    query, key, value = 0, 1, 2
    roles = [(query, key, value), (key, query, value), (key, value, query), (value, key, query)]
    for at in range(SQUARE):

        @pl.when(place == at)
        def _(at=at):
            kept, near, far = roles[at]
            chosen[kept] = kept_ref[...]
            chosen[near] = near_ref[...]
            first, last = (straight_ref, across_ref) if at % 2 == 0 else (across_ref, straight_ref)
            chosen[far, :, :unit] = first[...]
            chosen[far, :, unit:] = last[...]

    for start in range(0, kept_ref.shape[1], HS):
        head = slice(start, start + HS)
        scores = lax.dot_general(
            chosen[query, :, head], chosen[key, :, head], (((1,), (1,)), ((), ())), preferred_element_type=jnp.float32
        ) * (1.0 / math.sqrt(HS))
        weights = jnp.exp(scores - jnp.max(scores, axis=-1, keepdims=True))
        mass = jnp.sum(weights, axis=-1, keepdims=True)
        mixed = jnp.dot(weights.astype(jnp.bfloat16), chosen[value, :, head], preferred_element_type=jnp.float32)
        attended_ref[:, head] = (mixed / mass).astype(jnp.bfloat16)


def out_kernel(own_ref, *refs):
    got, (weight_ref, part_ref) = refs[:2], refs[2:]
    width = own_ref.shape[1]
    part = None
    for step, left in enumerate(arrange(own_ref, got)):
        rows = pl.ds(pl.multiple_of((pair_place() ^ step) * width, 128), width)
        term = jnp.dot(left, weight_ref[rows, :], preferred_element_type=jnp.float32)
        part = term if part is None else part + term
    part_ref[...] = part.astype(jnp.bfloat16)


def join_kernel(part_ref, core_ref, beside_ref, beside_core_ref, joined_ref):
    width = part_ref.shape[1]
    own = (part_ref[...].astype(jnp.float32) + core_ref[...].astype(jnp.float32)).astype(jnp.bfloat16)
    beside = (beside_ref[...].astype(jnp.float32) + beside_core_ref[...].astype(jnp.float32)).astype(jnp.bfloat16)
    odd = lax.rem(lax.axis_index("row"), 2) == 1
    joined_ref[:, :width] = jnp.where(odd, beside, own)
    joined_ref[:, width:] = jnp.where(odd, own, beside)


def resid_kernel(own_ref, *refs):
    got, (stream_ref, scale_ref, scaled_ref, squares_ref, tokens_ref, resid, blocks) = refs[:2], refs[2:]
    width = own_ref.shape[1]
    for step, added in enumerate(arrange(own_ref, got)):
        columns = pl.ds(pl.multiple_of((pair_place() ^ step) * width, 128), width)
        resid[:, columns] = stream_ref[:, columns] + added.astype(jnp.float32)
    whole = resid[...]
    scaled_ref[...] = (whole * scale_ref[...][None, :]).astype(jnp.bfloat16)
    squares_ref[...] = lanes(jnp.sum(whole * whole, axis=-1, keepdims=True))
    count, rows, _ = blocks.shape
    for block in range(count):
        blocks[block] = whole[rows * block : rows * (block + 1)]
    tokens_ref[...] = blocks[lax.axis_index("row")]


def down_kernel(columns, *refs):
    gate_ref, gate_other_ref, up_ref, up_other_ref, squares_ref, squares_other_ref, weight_ref, blocks_ref, hidden = refs
    inverse = factor(squares_ref, squares_other_ref)
    gate = (gate_ref[...] + gate_other_ref[...].astype(jnp.float32)) * inverse
    upward = (up_ref[...] + up_other_ref[...].astype(jnp.float32)) * inverse
    hidden[...] = (gate / (1.0 + jnp.exp(-gate)) * upward).astype(jnp.bfloat16)
    count, rows, _ = blocks_ref.shape
    for start in range(0, weight_ref.shape[1], columns):
        at = slice(start, start + columns)
        lowered = jnp.dot(hidden[...], weight_ref[:, at], preferred_element_type=jnp.float32)
        for block in range(count):
            blocks_ref[block, :, at] = lowered[rows * block : rows * (block + 1)].astype(jnp.bfloat16)


def leave_kernel(tokens_ref, blocks_ref, updated_ref):
    total = tokens_ref[...]
    for block in range(blocks_ref.shape[0]):
        total = total + blocks_ref[block].astype(jnp.float32)
    updated_ref[...] = total.astype(jnp.bfloat16)


def few_rows(hidden_states, scale_attn, w_qkv, w_out, scale_mlp, w_gate, w_up, w_down):
    bf16, f32 = jnp.bfloat16, jnp.float32
    tok_rows, half = hidden_states.shape
    count = lax.axis_size("row")
    tokens = tok_rows * count

    along = [from_row(hidden_states, 2 * step) for step in range(1, count // 2)]
    [own] = call(bring_kernel, [(hidden_states.shape, bf16)], hidden_states)
    [column] = call(pair_kernel, [((count // 2, tok_rows, half), bf16)], own, *along)
    pairs = [column, from_row(column, 1)]
    [scale_attn] = call(scale_kernel, [(scale_attn.shape, f32)], scale_attn, column)
    stream, scaled, squares = call(
        enter_kernel,
        [((tokens, half), f32), ((tokens, half), bf16), ((tokens, 128), f32)],
        *pairs, scale_attn,
        scratch=[pltpu.VMEM((count, tok_rows, half), f32)],
    )
    squares_other = other_core(squares)
    columns = w_qkv.shape[1]
    part, sent = call(functools.partial(product_kernel, 256), [((tokens, columns), f32), ((tokens, columns), bf16)], scaled, w_qkv)
    unit = columns // 3
    block, double = ((tokens, unit), bf16), ((tokens, 2 * unit), bf16)
    near, far = call(units_kernel, [double, block], part, other_core(sent), squares, squares_other)
    [attended] = call(
        attend_kernel, [double], near, from_row(near, 1), from_row(far, 2), from_row(far, 3),
        scratch=[pltpu.VMEM((3, tokens, 2 * unit), bf16)],
    )
    [part] = call(out_kernel, [block], attended, *spread(attended), w_out)
    across = lax.ppermute(part, ("row", "col"), [(i, i ^ 3) for i in range(2 * count)])
    [joined] = call(join_kernel, [double], part, other_core(part), from_row(part, 1), across, flops=10 * 10**8)
    scaled, squares, own = call(
        resid_kernel,
        [((tokens, half), bf16), ((tokens, 128), f32), ((tok_rows, half), f32)],
        joined, *spread(joined), stream, scale_mlp,
        flops=5 * 10**8,
        scratch=[pltpu.VMEM((tokens, half), f32), pltpu.VMEM((count, tok_rows, half), f32)],
    )
    squares_other = other_core(squares)
    units = w_gate.shape[1]
    product = functools.partial(product_kernel, 256)
    parts = [((tokens, units), f32), ((tokens, units), bf16)]
    gate, gate_sent = call(product, parts, scaled, w_gate)
    gate_other = other_core(gate_sent)
    upward, up_sent = call(product, parts, scaled, w_up)
    [lowered] = call(
        functools.partial(down_kernel, 256),
        [((count, tok_rows, half), bf16)],
        gate, gate_other, upward, other_core(up_sent), squares, squares_other, w_down,
        scratch=[pltpu.VMEM((tokens, units), bf16)],
    )
    lowered = lax.all_to_all(lowered, "row", split_axis=0, concat_axis=0, tiled=True)
    [updated] = call(leave_kernel, [((tok_rows, half), bf16)], own, lowered)
    return updated


def body(*arrays):
    fits = lax.axis_size("col") == 2 and lax.axis_size("row") == 2 * SQUARE and HEADS % (2 * SQUARE) == 0
    return (few_rows if fits else per_device)(*arrays)


def solution(mesh):
    return jax.shard_map(
        body,
        mesh=mesh,
        in_specs=(
            P(("groups", "row"), "col"),
            P("col"),
            P("col", "row"),
            P("col", "row"),
            P("col"),
            P("col", "row"),
            P("col", "row"),
            P("row", "col"),
        ),
        out_specs=P(("groups", "row"), "col"),
        check_vma=False,
    )
```
